128 devices in a mesh: worker: 4 (over x_lo, core), fsdp: 32 (over x_hi, y, z).
Axes of the slice: x: 4 (x_hi: 2, x_lo: 2; x = x_hi * 2 + x_lo), y: 4, z: 4, core: 2. Of those that a mesh axis runs over, the one named last changes fastest.
Arguments:
- out_grad: bfloat16 [65536, 4096], P(('worker', 'fsdp')), may hold values from -0.1875 to 0.1875
- hidden: bfloat16 [65536, 2048], P(('worker', 'fsdp')), may hold values from -6 to 6
- inner_param: float32 [4, 4096, 2048], P('worker', 'fsdp'), may hold values from -6 to 6
- adam_m: float32 [4, 4096, 2048], P('worker', 'fsdp'), may hold values from -6 to 6
- adam_v: float32 [4, 4096, 2048], P('worker', 'fsdp'), may hold values from 0.25 to 4
- old_inner: float32 [4, 4096, 2048], P('worker', 'fsdp'), may hold values from -6 to 6
- outer_param: float32 [4096, 2048], P('fsdp', 'worker'), may hold values from -6 to 6
- outer_mom: float32 [4096, 2048], P('fsdp', 'worker'), may hold values from -6 to 6
Outputs:
- param_next: float32 [4, 4096, 2048], P('worker', 'fsdp')
- first_next: float32 [4, 4096, 2048], P('worker', 'fsdp')
- second_next: float32 [4, 4096, 2048], P('worker', 'fsdp')
- outer_next: float32 [4096, 2048], P('fsdp', 'worker')
- moment_next: float32 [4096, 2048], P('fsdp', 'worker')
The draws below stay inside these ranges and needn't reach their ends.
All inputs are finite; a program needn't handle non-finite values.
Results may differ from the reference program's by a relative error of at most 0.0003.
Values may be sent and summed in bfloat16 or wider, within the bound.
A program may use at most 192 MiB of HBM per device.

```python
import math
import jax
import jax.numpy as jnp
from jax import lax

D = 4096
FRAG = 2048
TOK_DEV = 512
WORKERS = 4
TOKENS = 65536
N_WORKER = 4
N_FSDP = 32


def raised(drawn, stream_key, source, target, shards_of, factor):
    owner, partner = [(jnp.arange(drawn.shape[position]) // (drawn.shape[position] // shards_of)).reshape([-1 if axis == position else 1 for axis in range(drawn.ndim)]) for position in (source, target)]
    chosen = jax.random.permutation(stream_key, shards_of)[partner]
    strong = (owner == chosen) | (owner == (partner + shards_of // 2) % shards_of)
    return jnp.where(strong, factor * drawn, drawn)


def block_levels(rng, extent, shards, least, top_value):
    gain, own = 1.0, jax.random.fold_in(rng, 6)
    for dim, blocks in shards:
        draws = jnp.exp(jax.random.uniform(jax.random.fold_in(own, dim), (blocks,), jnp.float32, least / len(shards), top_value / len(shards)))
        gain = gain * jnp.repeat(draws, extent[dim] // blocks).reshape([-1 if axis == dim else 1 for axis in range(len(extent))])
    return gain


def normal_values(key, shape, spread, most, pieces=(), held_as=jnp.bfloat16):
    drawn = jax.random.normal(key, shape, jnp.float32) * spread
    if len(pieces) > 0:
        drawn = block_levels(key, shape, pieces, -0.22, 0.18) * drawn
    return jnp.clip(drawn, min=-most, max=most).astype(held_as)


def bell_draw_with(stream_key, extent, scale, reach, cuts, heavy, kind=jnp.bfloat16):
    entries = scale * jax.random.normal(stream_key, extent, jnp.float32)
    if cuts:
        entries = entries * block_levels(stream_key, extent, cuts, -0.22, 0.18)
    return jnp.clip(raised(entries, jax.random.fold_in(stream_key, 3), *heavy), -reach, reach).astype(kind)


def setup_inputs(seed: int = 0) -> dict:
    keys = jax.random.split(jax.random.key(seed), 9)
    return {
        "out_grad": bell_draw_with(keys[0], (TOKENS, D), (TOK_DEV * N_FSDP) ** -0.5, 0.1875, ((0, 128),), (0, 1, 128, 5.5)),
        "hidden": normal_values(keys[1], (TOKENS, FRAG), 1.0, 6.0, ((0, 128),)),
        "inner_param": normal_values(keys[2], (WORKERS, D, FRAG), 1.0, 6.0, ((0, 4), (1, 32)), jnp.float32),
        "adam_m": normal_values(keys[3], (WORKERS, D, FRAG), 1.0, 6.0, ((0, 4), (1, 32)), jnp.float32),
        "adam_v": jnp.clip(jnp.exp(math.log(4.0) - 2.7725887 * jax.random.uniform(keys[4], (WORKERS, D, FRAG), jnp.float32) ** block_levels(keys[4], (WORKERS, D, FRAG), ((0, 4), (1, 32)), -0.2, 0.2)), 0.25, 4.0),
        "old_inner": normal_values(keys[5], (WORKERS, D, FRAG), 1.0, 6.0, ((0, 4), (1, 32)), jnp.float32),
        "outer_param": normal_values(keys[6], (D, FRAG), 1.0, 6.0, ((0, 32), (1, 4)), jnp.float32),
        "outer_mom": normal_values(keys[7], (D, FRAG), 1.0, 6.0, ((0, 32), (1, 4)), jnp.float32),
    }


beta_one = 0.9
beta_two = 0.95
inner_step = 11
adam_eps = 1e-08
inner_rate = 0.3
decay_rate = 0.1
outer_rate = 0.7
outer_moment = 0.9

def worker_gradient(operands):
    grad_shards, act_shards = operands

    def add_shard(total, item):
        grad_shard, act_shard = item
        partial_sum = jnp.dot(grad_shard.astype(jnp.float32).T, act_shard.astype(jnp.float32), preferred_element_type=jnp.float32)
        return (total + partial_sum, None)
    start_total = jnp.zeros((D, FRAG), jnp.float32)
    total, unused = lax.scan(add_shard, start_total, (grad_shards, act_shards))
    return total

def adam_step(param, first_moment, second_moment, gradient):
    first_new = beta_one * first_moment + (1.0 - beta_one) * gradient
    second_new = beta_two * second_moment + (1.0 - beta_two) * gradient * gradient
    first_hat = first_new / (1.0 - beta_one ** inner_step)
    second_hat = second_new / (1.0 - beta_two ** inner_step)
    param_new = param - inner_rate * (first_hat / (jnp.sqrt(second_hat) + adam_eps) + decay_rate * param)
    return (param_new, first_new, second_new)

def nesterov(outer_param, outer_mom, outer_delta):
    moment_new = outer_moment * outer_mom + outer_delta
    outer_new = outer_param - outer_rate * (outer_delta + outer_moment * moment_new)
    return (outer_new, moment_new)

def reference(out_grad, hidden, inner_param, adam_m, adam_v, old_inner, outer_param, outer_mom):
    grad_blocks = out_grad.reshape(N_WORKER, N_FSDP, TOK_DEV, D)
    act_blocks = hidden.reshape(N_WORKER, N_FSDP, TOK_DEV, FRAG)
    gradient = lax.map(worker_gradient, (grad_blocks, act_blocks))
    param_next, first_next, second_next = adam_step(inner_param, adam_m, adam_v, gradient)
    outer_delta = outer_param - lax.optimization_barrier(jnp.sum(old_inner, axis=0)) * (1.0 / N_WORKER)
    outer_next, moment_next = nesterov(outer_param, outer_mom, outer_delta)
    return (param_next, first_next, second_next, outer_next, moment_next)
```

```python
import functools

import jax
import jax.numpy as jnp
from jax import lax
from jax.experimental import pallas as pl
from jax.experimental.pallas import tpu as pltpu
from jax.sharding import PartitionSpec as P

beta_one = 0.9
beta_two = 0.95
inner_step = 11
adam_eps = 1e-08
inner_rate = 0.3
decay_rate = 0.1
outer_rate = 0.7
outer_moment = 0.9

MESH = pl.DeviceIdType.MESH
ROWS = 128
COLS = 2048
TOK = 512
SHARE = 512
WIDE = 1024
SIDE = 128
MAIN = WIDE - SIDE
EXTRA = 128
SPLIT = MAIN - EXTRA
HALF = ROWS // 2
ITEMS = ((1, 2), (1, 1), (1, 3), (1, 0), (0, 2), (0, 1), (0, 3), (0, 0))
N_ITEM = len(ITEMS)
PIECES = 4
PIECE = ROWS // PIECES
PRE_ORDER = ((10, 6), (14, 9, 11), (2, 8, 5), (7, 13, 15), (1, 3, 4, 12, 0))
SCHEDULE = (
    "F0", "P0", "F1", "P1", "F2", "P2", "S0", "P3", "F3", "S1", "P4", "O", "T0",
    "F4", "S2", "T1", "F5", "S3", "T2", "F6", "S4", "T3", "F7", "R", "S5", "T4",
    "S6", "T5", "S7", "T6", "Q", "U", "T7",
)


def rel(stream, dx, da, db):
    return dx * 16 + (da * 4 + db if stream == 0 else db * 4 + da)


def block_order():
    order = []
    for step in SCHEDULE:
        kind, number = step[0], int(step[1:] or 0)
        if kind == "P":
            order += [16 + r for r in PRE_ORDER[number]]
        elif kind in "FST":
            dx, db = ITEMS[number]
            for s in (0, 1):
                order += [rel(s, dx, da, db) for da in {"F": (2,), "S": (1, 3), "T": (0,)}[kind]]
    return list(dict.fromkeys(order))


def adam_step(param, first_moment, second_moment, gradient):
    first_new = beta_one * first_moment + (1.0 - beta_one) * gradient
    second_new = beta_two * second_moment + (1.0 - beta_two) * gradient * gradient
    first_hat = first_new / (1.0 - beta_one**inner_step)
    second_hat = second_new / (1.0 - beta_two**inner_step)
    param_new = param - inner_rate * (
        first_hat / (jnp.sqrt(second_hat) + adam_eps) + decay_rate * param
    )
    return (param_new, first_new, second_new)


def nesterov(outer_param, outer_mom, outer_delta):
    moment_new = outer_moment * outer_mom + outer_delta
    outer_new = outer_param - outer_rate * (outer_delta + outer_moment * moment_new)
    return (outer_new, moment_new)


def encode(value):
    value = value * jnp.abs(value)
    return (value * jnp.abs(value)).astype(jnp.bfloat16)


def signed_root(value):
    return value * lax.rsqrt(jnp.maximum(jnp.abs(value), 1e-30))


def decode(code):
    return signed_root(signed_root(code.astype(jnp.float32)))


def kernel(
    a_hbm,
    b_hbm,
    old_hbm,
    p_hbm,
    m_hbm,
    v_hbm,
    op_hbm,
    om_hbm,
    pn_ref,
    mn_ref,
    vn_ref,
    on_ref,
    omn_ref,
    a_ref,
    b_ref,
    bx_ref,
    at_ref,
    own_ref,
    peers_ref,
    pair_ref,
    last_ref,
    state_ref,
    ostate_ref,
    pre_out,
    pre_in,
    pre_sum,
    extra_out,
    extra_in,
    s1_out0,
    s1_in0,
    s1_out1,
    s1_in1,
    m2_out0,
    m2_in0,
    m2_out1,
    m2_in1,
    x_out,
    x_in,
    t1_out,
    t1_in,
    t2_out,
    t2_in,
    load_sem,
    a_sem,
    state_sem,
    ostate_sem,
    p_ss,
    p_rs,
    s1_ss,
    s1_rs,
    m2_ss,
    m2_rs,
    x_ss,
    x_rs,
    t1_ss,
    t1_rs,
    t2_ss,
    t2_rs,
    o_ss,
    o_rs,
    l_ss,
    l_rs,
    e_ss,
    e_rs,
):
    s1_out, s1_in = (s1_out0, s1_out1), (s1_in0, s1_in1)
    m2_out, m2_in = (m2_out0, m2_out1), (m2_in0, m2_in1)
    w = lax.axis_index("worker")
    f = lax.axis_index("fsdp")
    px, py, pz = f // 16, (f // 4) % 4, f % 4

    def place(dx, dy, dz):
        return ((px + dx) % 2) * 16 + ((py + dy) % 4) * 4 + (pz + dz) % 4

    def near(stream, axis, way):
        along_y = (stream == 0) == (axis == 0)
        return (w, place(0, way, 0) if along_y else place(0, 0, way))

    across = (w, place(1, 0, 0))
    sibling, beside = (w // 2 * 2 + 1 - w % 2, f), ((w + 2) % 4, f)

    def strip(r):
        start = place(r // 16, (r // 4) % 4, r % 4) * ROWS
        return pl.ds(pl.multiple_of(start, ROWS), ROWS)

    loads = {
        r: pltpu.make_async_copy(a_hbm.at[:, strip(r)], a_ref.at[r], a_sem.at[r])
        for r in block_order()
    }
    b_loads = [
        pltpu.make_async_copy(
            b_hbm.at[:, pl.ds(s * WIDE, WIDE)], b_ref.at[s], load_sem.at[s]
        )
        for s in (0, 1)
    ]
    waiting = list(loads.values())
    for load in waiting[:1] + b_loads:
        load.start()

    barrier = pltpu.get_barrier_semaphore()
    friends = [near(0, 0, 1), near(0, 0, 3), near(1, 0, 1), near(1, 0, 3), across, sibling, beside]
    for friend in friends:
        pl.semaphore_signal(barrier, inc=1, device_id=friend, device_id_type=MESH)
    for load in waiting[1:]:
        load.start()
    pl.semaphore_wait(barrier, len(friends))

    started = []

    def send(src, dst, ssem, rsem, device):
        copy = pltpu.make_async_remote_copy(
            src_ref=src,
            dst_ref=dst,
            send_sem=ssem,
            recv_sem=rsem,
            device_id=device,
            device_id_type=MESH,
        )
        copy.start()
        started.append(copy)
        return copy

    def drain(keep):
        done = started[:keep]
        for copy in done:
            copy.wait_send()
        del started[: len(done)]

    turned = set()

    def turn(r):
        if r not in turned:
            turned.add(r)
            loads[r].wait()
            at_ref[r] = a_ref[r].T

    def product(r, columns):
        turn(r)
        return jnp.dot(at_ref[r], columns, preferred_element_type=jnp.float32)

    loaded = set()

    def right(s, lo, hi):
        if s not in loaded:
            loaded.add(s)
            b_loads[s].wait()
        return b_ref[s, :, lo:hi]

    def parts(s, dx, da, db, split=False):
        r = rel(s, dx, da, db)
        for lo, hi in ((0, SPLIT), (SPLIT, MAIN)) if split else ((0, MAIN),):
            yield pl.ds(lo, hi - lo), product(r, right(s, lo, hi))
        if dx == 0:
            pre_ready(r)
            yield pl.ds(MAIN, SIDE), pre_sum[r, :, s * SIDE : (s + 1) * SIDE]

    pre, summed_pre = {}, set()

    def pre_send(batch):
        if batch == 0:
            for s in (0, 1):
                bx_ref[:, s * SIDE : (s + 1) * SIDE] = right(s, MAIN, WIDE)
        for r in PRE_ORDER[batch]:
            pre_out[r] = encode(product(16 + r, bx_ref[...]))
            pre[r] = send(pre_out.at[r], pre_in.at[r], p_ss.at[r], p_rs.at[r], across)

    def pre_ready(r):
        if r not in summed_pre:
            summed_pre.add(r)
            pre[r].wait_recv()
            pre_sum[r] = product(r, bx_ref[...]) + decode(pre_in[r])

    s1, m2, xs, t1, t2, last, extra = {}, {}, {}, {}, {}, {}, {}

    def top(d):
        return slice(d * HALF, (d + 1) * HALF)

    def piece(h):
        return pl.ds(h * PIECE, PIECE)

    def first(k):
        dx, db = ITEMS[k]
        width = SPLIT if (dx, db) == (1, 0) else MAIN + (1 - dx) * SIDE
        for s in (0, 1):
            for cols, value in parts(s, dx, 2, db, db == 0):
                if db == 0 and cols.start == SPLIT:
                    if dx == 1:
                        extra_out[s] = encode(value)
                        extra[s] = send(
                            extra_out.at[s], extra_in.at[s], e_ss.at[s], e_rs.at[s], across
                        )
                        continue
                    extra[s].wait_recv()
                    value += decode(extra_in[s])
                for d in (0, 1):
                    s1_out[dx][s, db, d, :, cols] = encode(value[top(d)])
            for d in (0, 1):
                s1[s, k, d] = send(
                    s1_out[dx].at[s, db, d, :, pl.ds(0, width)],
                    s1_in[dx].at[s, db, d, :, pl.ds(0, width)],
                    s1_ss.at[s, k, d],
                    s1_rs.at[s, k, d],
                    near(s, 0, 3 if d else 1),
                )

    def second(k):
        dx, db = ITEMS[k]
        for s in (0, 1):
            for d in (0, 1):
                s1[s, k, d].wait_recv()
                split = (dx, db) == (1, 0)
                for cols, value in parts(s, dx, 3 if d else 1, db, split):
                    if split and cols.start == SPLIT:
                        m2_out[dx][s, db, d, :, cols] = encode(value)
                        continue
                    came = decode(s1_in[dx][s, db, d, :, cols])
                    m2_out[dx][s, db, d, top(d), cols] = encode(value[top(d)] + came)
                    m2_out[dx][s, db, d, top(1 - d), cols] = encode(value[top(1 - d)])
                if k == N_ITEM - 1:
                    for h in range(PIECES):
                        last[s, d, h] = send(
                            m2_out[dx].at[s, db, d, piece(h)],
                            m2_in[dx].at[s, db, d, piece(h)],
                            l_ss.at[s, d, h],
                            l_rs.at[s, d, h],
                            near(s, 0, 3 if d else 1),
                        )
                    continue
                m2[s, k, d] = send(
                    m2_out[dx].at[s, db, d],
                    m2_in[dx].at[s, db, d],
                    m2_ss.at[s, k, d],
                    m2_rs.at[s, k, d],
                    near(s, 0, 3 if d else 1),
                )

    def third(k):
        dx, db = ITEMS[k]
        for s in (0, 1):
            for d in (0, 1):
                m2[s, k, d].wait_recv()
            if dx == 0:
                xs[s, db].wait_recv()
            if dx == 0 and db in (1, 3):
                t1[s, db // 2].wait_recv()
            for cols, total in parts(s, dx, 0, db):
                total += decode(m2_in[dx][s, db, 0, :, cols])
                total += decode(m2_in[dx][s, db, 1, :, cols])
                if dx == 1:
                    x_out[s, db, :, cols] = encode(total)
                    continue
                if cols.start < MAIN:
                    total += decode(x_in[s, db, :, cols])
                if db == 2:
                    for d in (0, 1):
                        t1_out[s, d, :, cols] = encode(total[top(d)])
                else:
                    d = db // 2
                    came = decode(t1_in[s, d, :, cols])
                    t2_out[s, d, top(d), cols] = encode(total[top(d)] + came)
                    t2_out[s, d, top(1 - d), cols] = encode(total[top(1 - d)])
            if dx == 1:
                xs[s, db] = send(
                    x_out.at[s, db], x_in.at[s, db], x_ss.at[s, db], x_rs.at[s, db], across
                )
            elif db == 2:
                for d in (0, 1):
                    t1[s, d] = send(
                        t1_out.at[s, d],
                        t1_in.at[s, d],
                        t1_ss.at[s, d],
                        t1_rs.at[s, d],
                        near(s, 1, 3 if d else 1),
                    )
            else:
                d = db // 2
                for h in range(PIECES):
                    t2[s, d, h] = send(
                        t2_out.at[s, d, piece(h)],
                        t2_in.at[s, d, piece(h)],
                        t2_ss.at[s, d, h],
                        t2_rs.at[s, d, h],
                        near(s, 1, 3 if d else 1),
                    )

    def prepare():
        drain(-8 * PIECES)
        for s in (0, 1):
            xs[s, 0].wait_recv()
            for cols, value in parts(s, 0, 0, 0):
                if cols.start < MAIN:
                    value += decode(x_in[s, 0, :, cols])
                last_ref[s, :, cols] = value

    def finish():
        for h in range(PIECES):
            for s in (0, 1):
                for d in (0, 1):
                    t2[s, d, h].wait_recv()
                    last[s, d, h].wait_recv()
                total = last_ref[s, piece(h)]
                for d in (0, 1):
                    total += decode(t2_in[s, d, piece(h)])
                    total += decode(m2_in[0][s, 0, d, piece(h)])
                where = pl.ds(s * WIDE, WIDE)
                new = adam_step(*(state_ref[i, piece(h), where] for i in range(3)), total)
                for out, part in zip((pn_ref, mn_ref, vn_ref), new):
                    out[piece(h), where] = part

    core, chip = w % 2, w // 2
    outer = {}

    def share(worker):
        return old_hbm.at[:, pl.ds(pl.multiple_of(worker * SHARE, SHARE), SHARE)]

    own_loads = [
        pltpu.make_async_copy(share(w), own_ref.at[0], load_sem.at[2]),
        pltpu.make_async_copy(share((w + 2) % 4), own_ref.at[1], load_sem.at[3]),
    ]

    outer_loads = [
        pltpu.make_async_copy(src, ostate_ref.at[i], ostate_sem.at[i])
        for i, src in enumerate((op_hbm, om_hbm))
    ]
    state_loads = [
        pltpu.make_async_copy(src, state_ref.at[i], state_sem.at[i])
        for i, src in enumerate((p_hbm, m_hbm, v_hbm))
    ]

    def outer_send():
        for load in outer_loads + state_loads:
            load.start()
        for load in own_loads:
            load.start()
        for i in (0, 1):
            outer[i] = send(
                share((chip + i) % 2 * 2 + 1 - core), peers_ref.at[i], o_ss.at[i], o_rs.at[i], sibling
            )

    def outer_pass():
        for load in own_loads:
            load.wait()
        outer[1].wait_recv()
        pair_ref[...] = own_ref[1] + peers_ref[1]
        outer[2] = send(pair_ref, peers_ref.at[2], o_ss.at[2], o_rs.at[2], beside)

    def outer_sum():
        outer[0].wait_recv()
        outer[2].wait_recv()
        share_sum = (own_ref[0] + peers_ref[0]) + peers_ref[2]
        for load in outer_loads:
            load.wait()
        outer_delta = ostate_ref[0] - share_sum * (1.0 / 4)
        on_ref[...], omn_ref[...] = nesterov(ostate_ref[0], ostate_ref[1], outer_delta)
        for load in state_loads:
            load.wait()

    steps = {"F": first, "S": second, "T": third, "P": pre_send}
    for step in SCHEDULE:
        if step == "O":
            outer_send()
        elif step == "U":
            prepare()
        elif step == "T7":
            finish()
        elif step == "R":
            outer_pass()
        elif step == "Q":
            outer_sum()
        else:
            steps[step[0]](int(step[1:]))
    drain(None)


def step_all(out_grad, hidden, old_inner, *state):
    bf16, f32 = jnp.bfloat16, jnp.float32
    dma = pltpu.SemaphoreType.DMA
    anywhere = pl.BlockSpec(memory_space=pl.ANY)
    full = pltpu.VMEM((ROWS, COLS), f32)
    part = pltpu.VMEM((ROWS, SHARE), f32)
    return pl.pallas_call(
        kernel,
        out_shape=(full, full, full, part, part),
        in_specs=[anywhere] * 8,
        out_specs=(pl.BlockSpec(memory_space=pltpu.VMEM),) * 5,
        scratch_shapes=[
            pltpu.VMEM((32, TOK, ROWS), bf16),
            pltpu.VMEM((2, TOK, WIDE), bf16),
            pltpu.VMEM((TOK, 2 * SIDE), bf16),
            pltpu.VMEM((32, ROWS, TOK), bf16),
            pltpu.VMEM((2, ROWS, SHARE), f32),
            pltpu.VMEM((3, ROWS, SHARE), f32),
            pltpu.VMEM((ROWS, SHARE), f32),
            pltpu.VMEM((2, ROWS, WIDE), f32),
            pltpu.VMEM((3, ROWS, COLS), f32),
            pltpu.VMEM((2, ROWS, SHARE), f32),
            pltpu.VMEM((16, ROWS, 2 * SIDE), bf16),
            pltpu.VMEM((16, ROWS, 2 * SIDE), bf16),
            pltpu.VMEM((16, ROWS, 2 * SIDE), f32),
            pltpu.VMEM((2, ROWS, EXTRA), bf16),
            pltpu.VMEM((2, ROWS, EXTRA), bf16),
            pltpu.VMEM((2, 4, 2, HALF, WIDE), bf16),
            pltpu.VMEM((2, 4, 2, HALF, WIDE), bf16),
            pltpu.VMEM((2, 4, 2, HALF, MAIN), bf16),
            pltpu.VMEM((2, 4, 2, HALF, MAIN), bf16),
            pltpu.VMEM((2, 4, 2, ROWS, WIDE), bf16),
            pltpu.VMEM((2, 4, 2, ROWS, WIDE), bf16),
            pltpu.VMEM((2, 4, 2, ROWS, MAIN), bf16),
            pltpu.VMEM((2, 4, 2, ROWS, MAIN), bf16),
            pltpu.VMEM((2, 4, ROWS, MAIN), bf16),
            pltpu.VMEM((2, 4, ROWS, MAIN), bf16),
            pltpu.VMEM((2, 2, HALF, WIDE), bf16),
            pltpu.VMEM((2, 2, HALF, WIDE), bf16),
            pltpu.VMEM((2, 2, ROWS, WIDE), bf16),
            pltpu.VMEM((2, 2, ROWS, WIDE), bf16),
            dma((4,)),
            dma((32,)),
            dma((3,)),
            dma((2,)),
            dma((16,)),
            dma((16,)),
            dma((2, N_ITEM, 2)),
            dma((2, N_ITEM, 2)),
            dma((2, N_ITEM, 2)),
            dma((2, N_ITEM, 2)),
            dma((2, 4)),
            dma((2, 4)),
            dma((2, 2)),
            dma((2, 2)),
            dma((2, 2, PIECES)),
            dma((2, 2, PIECES)),
            dma((3,)),
            dma((3,)),
            dma((2, 2, PIECES)),
            dma((2, 2, PIECES)),
            dma((2,)),
            dma((2,)),
        ],
        compiler_params=pltpu.CompilerParams(
            collective_id=0, has_side_effects=True, vmem_limit_bytes=53 << 20
        ),
        cost_estimate=pl.CostEstimate(
            flops=2 * TOK * 32 * ROWS * COLS, bytes_accessed=10 << 20, transcendentals=0
        ),
        name="step_all",
    )(out_grad, hidden, old_inner, *state)


def write_kernel(*refs):
    ins, outs, sem = refs[:5], refs[5:10], refs[10]
    copies = [
        pltpu.make_async_copy(src, dst, sem.at[i]) for i, (src, dst) in enumerate(zip(ins, outs))
    ]
    for copy in copies:
        copy.start()
    for copy in copies:
        copy.wait()


def write_all(results):
    anywhere = pl.BlockSpec(memory_space=pl.ANY)
    return pl.pallas_call(
        write_kernel,
        out_shape=tuple(pltpu.HBM(r.shape, r.dtype) for r in results),
        in_specs=[anywhere] * 5,
        out_specs=(anywhere,) * 5,
        scratch_shapes=[pltpu.SemaphoreType.DMA((5,))],
        compiler_params=pltpu.CompilerParams(vmem_limit_bytes=1 << 20),
        name="write_all",
    )(*(pltpu.with_memory_space_constraint(r, pltpu.VMEM) for r in results))


def per_device(out_grad, hidden, inner_param, adam_m, adam_v, old_inner, outer_param, outer_mom):
    results = step_all(
        out_grad, hidden, old_inner[0], inner_param[0], adam_m[0], adam_v[0], outer_param, outer_mom
    )
    param_next, first_next, second_next, outer_next, moment_next = write_all(results)
    return (param_next[None], first_next[None], second_next[None], outer_next, moment_next)


def solution(mesh):
    in_specs = (
        P(("worker", "fsdp"), None),
        P(("worker", "fsdp"), None),
        P("worker", "fsdp", None),
        P("worker", "fsdp", None),
        P("worker", "fsdp", None),
        P("worker", "fsdp", None),
        P("fsdp", "worker"),
        P("fsdp", "worker"),
    )
    out_specs = (
        P("worker", "fsdp", None),
        P("worker", "fsdp", None),
        P("worker", "fsdp", None),
        P("fsdp", "worker"),
        P("fsdp", "worker"),
    )
    return jax.shard_map(
        per_device, mesh=mesh, in_specs=in_specs, out_specs=out_specs, check_vma=False
    )
```

```python
import functools

import jax
import jax.numpy as jnp
from jax import lax
from jax.experimental import pallas as pl
from jax.experimental.pallas import tpu as pltpu
from jax.sharding import PartitionSpec as P

beta_one = 0.9
beta_two = 0.95
inner_step = 11
adam_eps = 1e-08
inner_rate = 0.3
decay_rate = 0.1
outer_rate = 0.7
outer_moment = 0.9

MESH = pl.DeviceIdType.MESH
ROWS = 128
COLS = 2048
TOK = 512
SHARE = 512
WIDE = 1024
SIDE = 128
MAIN = WIDE - SIDE
EXTRA = 128
SPLIT = MAIN - EXTRA
HALF = ROWS // 2
ITEMS = ((1, 2), (1, 1), (1, 3), (1, 0), (0, 2), (0, 1), (0, 3), (0, 0))
N_ITEM = len(ITEMS)
PIECES = 2
PIECE = ROWS // PIECES
PRE_ORDER = ((10, 6), (14, 9, 11), (2, 8, 5), (7, 13, 15), (1, 3, 4, 12, 0))
SCHEDULE = (
    "F0", "P0", "F1", "P1", "F2", "P2", "S0", "P3", "F3", "S1", "P4", "O", "T0",
    "F4", "S2", "T1", "F5", "S3", "T2", "F6", "S4", "T3", "F7", "R", "S5", "T4",
    "S6", "T5", "S7", "T6", "Q", "U", "T7",
)


def rel(stream, dx, da, db):
    return dx * 16 + (da * 4 + db if stream == 0 else db * 4 + da)


def block_order():
    order = []
    for step in SCHEDULE:
        kind, number = step[0], int(step[1:] or 0)
        if kind == "P":
            order += [16 + r for r in PRE_ORDER[number]]
        elif kind in "FST":
            dx, db = ITEMS[number]
            for s in (0, 1):
                order += [rel(s, dx, da, db) for da in {"F": (2,), "S": (1, 3), "T": (0,)}[kind]]
    return list(dict.fromkeys(order))


def adam_step(param, first_moment, second_moment, gradient):
    first_new = beta_one * first_moment + (1.0 - beta_one) * gradient
    second_new = beta_two * second_moment + (1.0 - beta_two) * gradient * gradient
    first_hat = first_new / (1.0 - beta_one**inner_step)
    second_hat = second_new / (1.0 - beta_two**inner_step)
    param_new = param - inner_rate * (
        first_hat / (jnp.sqrt(second_hat) + adam_eps) + decay_rate * param
    )
    return (param_new, first_new, second_new)


def nesterov(outer_param, outer_mom, outer_delta):
    moment_new = outer_moment * outer_mom + outer_delta
    outer_new = outer_param - outer_rate * (outer_delta + outer_moment * moment_new)
    return (outer_new, moment_new)


def encode(value):
    value = value * jnp.abs(value)
    return (value * jnp.abs(value)).astype(jnp.bfloat16)


def signed_root(value):
    return value * lax.rsqrt(jnp.maximum(jnp.abs(value), 1e-30))


def decode(code):
    return signed_root(signed_root(code.astype(jnp.float32)))


def kernel(
    a_hbm,
    b_hbm,
    old_hbm,
    p_hbm,
    m_hbm,
    v_hbm,
    op_hbm,
    om_hbm,
    pn_ref,
    mn_ref,
    vn_ref,
    on_ref,
    omn_ref,
    a_ref,
    b_ref,
    bx_ref,
    at_ref,
    own_ref,
    peers_ref,
    pair_ref,
    last_ref,
    state_ref,
    ostate_ref,
    pre_out,
    pre_in,
    pre_sum,
    extra_out,
    extra_in,
    s1_out0,
    s1_in0,
    s1_out1,
    s1_in1,
    m2_out0,
    m2_in0,
    m2_out1,
    m2_in1,
    x_out,
    x_in,
    t1_out,
    t1_in,
    t2_out,
    t2_in,
    load_sem,
    a_sem,
    state_sem,
    ostate_sem,
    p_ss,
    p_rs,
    s1_ss,
    s1_rs,
    m2_ss,
    m2_rs,
    x_ss,
    x_rs,
    t1_ss,
    t1_rs,
    t2_ss,
    t2_rs,
    o_ss,
    o_rs,
    l_ss,
    l_rs,
    e_ss,
    e_rs,
):
    s1_out, s1_in = (s1_out0, s1_out1), (s1_in0, s1_in1)
    m2_out, m2_in = (m2_out0, m2_out1), (m2_in0, m2_in1)
    w = lax.axis_index("worker")
    f = lax.axis_index("fsdp")
    px, py, pz = f // 16, (f // 4) % 4, f % 4

    def place(dx, dy, dz):
        return ((px + dx) % 2) * 16 + ((py + dy) % 4) * 4 + (pz + dz) % 4

    def near(stream, axis, way):
        along_y = (stream == 0) == (axis == 0)
        return (w, place(0, way, 0) if along_y else place(0, 0, way))

    across = (w, place(1, 0, 0))
    sibling, beside = (w // 2 * 2 + 1 - w % 2, f), ((w + 2) % 4, f)

    def strip(r):
        start = place(r // 16, (r // 4) % 4, r % 4) * ROWS
        return pl.ds(pl.multiple_of(start, ROWS), ROWS)

    loads = {
        r: pltpu.make_async_copy(a_hbm.at[:, strip(r)], a_ref.at[r], a_sem.at[r])
        for r in block_order()
    }
    b_loads = [
        pltpu.make_async_copy(
            b_hbm.at[:, pl.ds(s * WIDE, WIDE)], b_ref.at[s], load_sem.at[s]
        )
        for s in (0, 1)
    ]
    waiting = list(loads.values())
    for load in waiting[:1] + b_loads:
        load.start()

    barrier = pltpu.get_barrier_semaphore()
    friends = [near(0, 0, 1), near(0, 0, 3), near(1, 0, 1), near(1, 0, 3), across, sibling, beside]
    for friend in friends:
        pl.semaphore_signal(barrier, inc=1, device_id=friend, device_id_type=MESH)
    for load in waiting[1:]:
        load.start()
    pl.semaphore_wait(barrier, len(friends))

    started = []

    def send(src, dst, ssem, rsem, device):
        copy = pltpu.make_async_remote_copy(
            src_ref=src,
            dst_ref=dst,
            send_sem=ssem,
            recv_sem=rsem,
            device_id=device,
            device_id_type=MESH,
        )
        copy.start()
        started.append(copy)
        return copy

    def drain(keep):
        done = started[:keep]
        for copy in done:
            copy.wait_send()
        del started[: len(done)]

    turned = set()

    def turn(r):
        if r not in turned:
            turned.add(r)
            loads[r].wait()
            at_ref[r] = a_ref[r].T

    def product(r, columns):
        turn(r)
        return jnp.dot(at_ref[r], columns, preferred_element_type=jnp.float32)

    loaded = set()

    def right(s, lo, hi):
        if s not in loaded:
            loaded.add(s)
            b_loads[s].wait()
        return b_ref[s, :, lo:hi]

    def parts(s, dx, da, db, split=False):
        r = rel(s, dx, da, db)
        for lo, hi in ((0, SPLIT), (SPLIT, MAIN)) if split else ((0, MAIN),):
            yield pl.ds(lo, hi - lo), product(r, right(s, lo, hi))
        if dx == 0:
            pre_ready(r)
            yield pl.ds(MAIN, SIDE), pre_sum[r, :, s * SIDE : (s + 1) * SIDE]

    pre, summed_pre = {}, set()

    def pre_send(batch):
        if batch == 0:
            for s in (0, 1):
                bx_ref[:, s * SIDE : (s + 1) * SIDE] = right(s, MAIN, WIDE)
        for r in PRE_ORDER[batch]:
            pre_out[r] = encode(product(16 + r, bx_ref[...]))
            pre[r] = send(pre_out.at[r], pre_in.at[r], p_ss.at[r], p_rs.at[r], across)

    def pre_ready(r):
        if r not in summed_pre:
            summed_pre.add(r)
            pre[r].wait_recv()
            pre_sum[r] = product(r, bx_ref[...]) + decode(pre_in[r])

    s1, m2, xs, t1, t2, last, extra = {}, {}, {}, {}, {}, {}, {}

    def top(d):
        return slice(d * HALF, (d + 1) * HALF)

    def piece(h):
        return pl.ds(h * PIECE, PIECE)

    def first(k):
        dx, db = ITEMS[k]
        width = SPLIT if (dx, db) == (1, 0) else MAIN + (1 - dx) * SIDE
        for s in (0, 1):
            for cols, value in parts(s, dx, 2, db, db == 0):
                if db == 0 and cols.start == SPLIT:
                    if dx == 1:
                        extra_out[s] = encode(value)
                        extra[s] = send(
                            extra_out.at[s], extra_in.at[s], e_ss.at[s], e_rs.at[s], across
                        )
                        continue
                    extra[s].wait_recv()
                    value += decode(extra_in[s])
                for d in (0, 1):
                    s1_out[dx][s, db, d, :, cols] = encode(value[top(d)])
            for d in (0, 1):
                s1[s, k, d] = send(
                    s1_out[dx].at[s, db, d, :, pl.ds(0, width)],
                    s1_in[dx].at[s, db, d, :, pl.ds(0, width)],
                    s1_ss.at[s, k, d],
                    s1_rs.at[s, k, d],
                    near(s, 0, 3 if d else 1),
                )

    def second(k):
        dx, db = ITEMS[k]
        for s in (0, 1):
            for d in (0, 1):
                s1[s, k, d].wait_recv()
                split = (dx, db) == (1, 0)
                for cols, value in parts(s, dx, 3 if d else 1, db, split):
                    if split and cols.start == SPLIT:
                        m2_out[dx][s, db, d, :, cols] = encode(value)
                        continue
                    came = decode(s1_in[dx][s, db, d, :, cols])
                    m2_out[dx][s, db, d, top(d), cols] = encode(value[top(d)] + came)
                    m2_out[dx][s, db, d, top(1 - d), cols] = encode(value[top(1 - d)])
                if k == N_ITEM - 1:
                    for h in range(PIECES):
                        last[s, d, h] = send(
                            m2_out[dx].at[s, db, d, piece(h)],
                            m2_in[dx].at[s, db, d, piece(h)],
                            l_ss.at[s, d, h],
                            l_rs.at[s, d, h],
                            near(s, 0, 3 if d else 1),
                        )
                    continue
                m2[s, k, d] = send(
                    m2_out[dx].at[s, db, d],
                    m2_in[dx].at[s, db, d],
                    m2_ss.at[s, k, d],
                    m2_rs.at[s, k, d],
                    near(s, 0, 3 if d else 1),
                )

    def third(k):
        dx, db = ITEMS[k]
        for s in (0, 1):
            for d in (0, 1):
                m2[s, k, d].wait_recv()
            if dx == 0:
                xs[s, db].wait_recv()
            if dx == 0 and db in (1, 3):
                t1[s, db // 2].wait_recv()
            for cols, total in parts(s, dx, 0, db):
                total += decode(m2_in[dx][s, db, 0, :, cols])
                total += decode(m2_in[dx][s, db, 1, :, cols])
                if dx == 1:
                    x_out[s, db, :, cols] = encode(total)
                    continue
                if cols.start < MAIN:
                    total += decode(x_in[s, db, :, cols])
                if db == 2:
                    for d in (0, 1):
                        t1_out[s, d, :, cols] = encode(total[top(d)])
                else:
                    d = db // 2
                    came = decode(t1_in[s, d, :, cols])
                    t2_out[s, d, top(d), cols] = encode(total[top(d)] + came)
                    t2_out[s, d, top(1 - d), cols] = encode(total[top(1 - d)])
            if dx == 1:
                xs[s, db] = send(
                    x_out.at[s, db], x_in.at[s, db], x_ss.at[s, db], x_rs.at[s, db], across
                )
            elif db == 2:
                for d in (0, 1):
                    t1[s, d] = send(
                        t1_out.at[s, d],
                        t1_in.at[s, d],
                        t1_ss.at[s, d],
                        t1_rs.at[s, d],
                        near(s, 1, 3 if d else 1),
                    )
            else:
                d = db // 2
                for h in range(PIECES):
                    t2[s, d, h] = send(
                        t2_out.at[s, d, piece(h)],
                        t2_in.at[s, d, piece(h)],
                        t2_ss.at[s, d, h],
                        t2_rs.at[s, d, h],
                        near(s, 1, 3 if d else 1),
                    )

    def prepare():
        drain(-8 * PIECES)
        for s in (0, 1):
            xs[s, 0].wait_recv()
            for cols, value in parts(s, 0, 0, 0):
                if cols.start < MAIN:
                    value += decode(x_in[s, 0, :, cols])
                last_ref[s, :, cols] = value

    def finish():
        for h in range(PIECES):
            for s in (0, 1):
                for d in (0, 1):
                    t2[s, d, h].wait_recv()
                    last[s, d, h].wait_recv()
                total = last_ref[s, piece(h)]
                for d in (0, 1):
                    total += decode(t2_in[s, d, piece(h)])
                    total += decode(m2_in[0][s, 0, d, piece(h)])
                where = pl.ds(s * WIDE, WIDE)
                new = adam_step(*(state_ref[i, piece(h), where] for i in range(3)), total)
                for out, part in zip((pn_ref, mn_ref, vn_ref), new):
                    out[piece(h), where] = part

    core, chip = w % 2, w // 2
    outer = {}

    def share(worker):
        return old_hbm.at[:, pl.ds(pl.multiple_of(worker * SHARE, SHARE), SHARE)]

    own_loads = [
        pltpu.make_async_copy(share(w), own_ref.at[0], load_sem.at[2]),
        pltpu.make_async_copy(share((w + 2) % 4), own_ref.at[1], load_sem.at[3]),
    ]

    outer_loads = [
        pltpu.make_async_copy(src, ostate_ref.at[i], ostate_sem.at[i])
        for i, src in enumerate((op_hbm, om_hbm))
    ]
    state_loads = [
        pltpu.make_async_copy(src, state_ref.at[i], state_sem.at[i])
        for i, src in enumerate((p_hbm, m_hbm, v_hbm))
    ]

    def outer_send():
        for load in outer_loads + state_loads:
            load.start()
        for load in own_loads:
            load.start()
        for i in (0, 1):
            outer[i] = send(
                share((chip + i) % 2 * 2 + 1 - core), peers_ref.at[i], o_ss.at[i], o_rs.at[i], sibling
            )

    def outer_pass():
        for load in own_loads:
            load.wait()
        outer[1].wait_recv()
        pair_ref[...] = own_ref[1] + peers_ref[1]
        outer[2] = send(pair_ref, peers_ref.at[2], o_ss.at[2], o_rs.at[2], beside)

    def outer_sum():
        outer[0].wait_recv()
        outer[2].wait_recv()
        share_sum = (own_ref[0] + peers_ref[0]) + peers_ref[2]
        for load in outer_loads:
            load.wait()
        outer_delta = ostate_ref[0] - share_sum * (1.0 / 4)
        on_ref[...], omn_ref[...] = nesterov(ostate_ref[0], ostate_ref[1], outer_delta)
        for load in state_loads:
            load.wait()

    steps = {"F": first, "S": second, "T": third, "P": pre_send}
    for step in SCHEDULE:
        if step == "O":
            outer_send()
        elif step == "U":
            prepare()
        elif step == "T7":
            finish()
        elif step == "R":
            outer_pass()
        elif step == "Q":
            outer_sum()
        else:
            steps[step[0]](int(step[1:]))
    drain(None)


def step_all(out_grad, hidden, old_inner, *state):
    bf16, f32 = jnp.bfloat16, jnp.float32
    dma = pltpu.SemaphoreType.DMA
    anywhere = pl.BlockSpec(memory_space=pl.ANY)
    full = pltpu.VMEM((ROWS, COLS), f32)
    part = pltpu.VMEM((ROWS, SHARE), f32)
    return pl.pallas_call(
        kernel,
        out_shape=(full, full, full, part, part),
        in_specs=[anywhere] * 8,
        out_specs=(pl.BlockSpec(memory_space=pltpu.VMEM),) * 5,
        scratch_shapes=[
            pltpu.VMEM((32, TOK, ROWS), bf16),
            pltpu.VMEM((2, TOK, WIDE), bf16),
            pltpu.VMEM((TOK, 2 * SIDE), bf16),
            pltpu.VMEM((32, ROWS, TOK), bf16),
            pltpu.VMEM((2, ROWS, SHARE), f32),
            pltpu.VMEM((3, ROWS, SHARE), f32),
            pltpu.VMEM((ROWS, SHARE), f32),
            pltpu.VMEM((2, ROWS, WIDE), f32),
            pltpu.VMEM((3, ROWS, COLS), f32),
            pltpu.VMEM((2, ROWS, SHARE), f32),
            pltpu.VMEM((16, ROWS, 2 * SIDE), bf16),
            pltpu.VMEM((16, ROWS, 2 * SIDE), bf16),
            pltpu.VMEM((16, ROWS, 2 * SIDE), f32),
            pltpu.VMEM((2, ROWS, EXTRA), bf16),
            pltpu.VMEM((2, ROWS, EXTRA), bf16),
            pltpu.VMEM((2, 4, 2, HALF, WIDE), bf16),
            pltpu.VMEM((2, 4, 2, HALF, WIDE), bf16),
            pltpu.VMEM((2, 4, 2, HALF, MAIN), bf16),
            pltpu.VMEM((2, 4, 2, HALF, MAIN), bf16),
            pltpu.VMEM((2, 4, 2, ROWS, WIDE), bf16),
            pltpu.VMEM((2, 4, 2, ROWS, WIDE), bf16),
            pltpu.VMEM((2, 4, 2, ROWS, MAIN), bf16),
            pltpu.VMEM((2, 4, 2, ROWS, MAIN), bf16),
            pltpu.VMEM((2, 4, ROWS, MAIN), bf16),
            pltpu.VMEM((2, 4, ROWS, MAIN), bf16),
            pltpu.VMEM((2, 2, HALF, WIDE), bf16),
            pltpu.VMEM((2, 2, HALF, WIDE), bf16),
            pltpu.VMEM((2, 2, ROWS, WIDE), bf16),
            pltpu.VMEM((2, 2, ROWS, WIDE), bf16),
            dma((4,)),
            dma((32,)),
            dma((3,)),
            dma((2,)),
            dma((16,)),
            dma((16,)),
            dma((2, N_ITEM, 2)),
            dma((2, N_ITEM, 2)),
            dma((2, N_ITEM, 2)),
            dma((2, N_ITEM, 2)),
            dma((2, 4)),
            dma((2, 4)),
            dma((2, 2)),
            dma((2, 2)),
            dma((2, 2, PIECES)),
            dma((2, 2, PIECES)),
            dma((3,)),
            dma((3,)),
            dma((2, 2, PIECES)),
            dma((2, 2, PIECES)),
            dma((2,)),
            dma((2,)),
        ],
        compiler_params=pltpu.CompilerParams(
            collective_id=0, has_side_effects=True, vmem_limit_bytes=53 << 20
        ),
        cost_estimate=pl.CostEstimate(
            flops=2 * TOK * 32 * ROWS * COLS, bytes_accessed=10 << 20, transcendentals=0
        ),
        name="step_all",
    )(out_grad, hidden, old_inner, *state)


def write_kernel(*refs):
    ins, outs, sem = refs[:5], refs[5:10], refs[10]
    copies = [
        pltpu.make_async_copy(src, dst, sem.at[i]) for i, (src, dst) in enumerate(zip(ins, outs))
    ]
    for copy in copies:
        copy.start()
    for copy in copies:
        copy.wait()


def write_all(results):
    anywhere = pl.BlockSpec(memory_space=pl.ANY)
    return pl.pallas_call(
        write_kernel,
        out_shape=tuple(pltpu.HBM(r.shape, r.dtype) for r in results),
        in_specs=[anywhere] * 5,
        out_specs=(anywhere,) * 5,
        scratch_shapes=[pltpu.SemaphoreType.DMA((5,))],
        compiler_params=pltpu.CompilerParams(vmem_limit_bytes=1 << 20),
        name="write_all",
    )(*(pltpu.with_memory_space_constraint(r, pltpu.VMEM) for r in results))


def per_device(out_grad, hidden, inner_param, adam_m, adam_v, old_inner, outer_param, outer_mom):
    results = step_all(
        out_grad, hidden, old_inner[0], inner_param[0], adam_m[0], adam_v[0], outer_param, outer_mom
    )
    param_next, first_next, second_next, outer_next, moment_next = write_all(results)
    return (param_next[None], first_next[None], second_next[None], outer_next, moment_next)


def solution(mesh):
    in_specs = (
        P(("worker", "fsdp"), None),
        P(("worker", "fsdp"), None),
        P("worker", "fsdp", None),
        P("worker", "fsdp", None),
        P("worker", "fsdp", None),
        P("worker", "fsdp", None),
        P("fsdp", "worker"),
        P("fsdp", "worker"),
    )
    out_specs = (
        P("worker", "fsdp", None),
        P("worker", "fsdp", None),
        P("worker", "fsdp", None),
        P("fsdp", "worker"),
        P("fsdp", "worker"),
    )
    return jax.shard_map(
        per_device, mesh=mesh, in_specs=in_specs, out_specs=out_specs, check_vma=False
    )
```
